32 devices in a mesh: row: 4 (over z), col: 4 (over y, core), dp: 2 (over x).
Axes of the slice: x: 2, y: 2, z: 4, core: 2. Of those that a mesh axis runs over, the one named last changes fastest.
Arguments:
- grad_out: bfloat16 [2, 128, 8192], P('dp', 'row', 'col'), may hold values from -6 to 6
- gate_pre: bfloat16 [2, 128, 28672], P('dp', 'col', 'row'), may hold values from -6 to 6
- up_pre: bfloat16 [2, 128, 28672], P('dp', 'col', 'row'), may hold values from -6 to 6
- w_down: bfloat16 [28672, 8192], P('row', 'col'), may hold values from -0.046875 to 0.046875
- block_mask: int32 [224, 64], replicated, may hold values 0 or 1
Outputs:
- grad_gate: bfloat16 [2, 128, 28672], P('dp', 'col', 'row')
- grad_up: bfloat16 [2, 128, 28672], P('dp', 'col', 'row')
- grad_down: bfloat16 [28672, 8192], P('row', 'col')
The draws below stay inside these ranges and needn't reach their ends.
All inputs are finite; a program needn't handle non-finite values.
Results may differ from the reference program's by a relative error of at most 0.019.
Values may be sent and summed in bfloat16 or wider, within the bound.
No kernel may reach another device: no remote copies, remote signals or barrier semaphores. Data moves between devices by JAX's collectives and lax.ppermute only.
A program may use at most 256 MiB of HBM per device.

```python
import jax
import jax.numpy as jnp
from jax import lax

D = 8192
FF = 28672
BLOCK = 128
GROUP = 128
NFB = 224
NDB = 64
N_COL = 4
N_DP = 2


def place_ends(values, rng, least, largest):
    extent = values.shape
    index_at = [jax.random.randint(jax.random.fold_in(rng, axis), (), 0, extent[axis]) for axis in range(len(extent))]
    values = values.at[tuple(index_at)].set(least)
    longest = extent.index(max(extent))
    index_at[longest] = (index_at[longest] + 1) % extent[longest]
    return values.at[tuple(index_at)].set(largest)


def block_levels(key, extent, shards, low, top_value):
    factor_of, own = 1.0, jax.random.fold_in(key, 6)
    for position, shards_of in shards:
        draws = jnp.exp(jax.random.uniform(jax.random.fold_in(own, position), (shards_of,), jnp.float32, low / len(shards), top_value / len(shards)))
        factor_of = factor_of * jnp.repeat(draws, extent[position] // shards_of).reshape([-1 if axis == position else 1 for axis in range(len(extent))])
    return factor_of


def bell_draw(rng, shape, scale, bound, pieces=(), held_as=jnp.bfloat16):
    loudness = block_levels(rng, shape, pieces, -0.22, 0.18) if pieces else 1.0
    values = jax.random.normal(rng, shape, jnp.float32) * scale * loudness
    return jnp.minimum(jnp.maximum(values, -bound), bound).astype(held_as)


def setup_inputs(seed: int = 0) -> dict:
    keys = jax.random.split(jax.random.key(seed), 6)
    grad_out = bell_draw(keys[0], (N_DP, GROUP, D), 1.0, 6.0, ((0, 2), (1, 4), (2, 4)))
    gate_pre = bell_draw(keys[1], (N_DP, GROUP, FF), 1.5, 6.0, ((0, 2), (1, 4), (2, 4)))
    up_pre = bell_draw(keys[2], (N_DP, GROUP, FF), 1.0, 6.0, ((0, 2), (1, 4), (2, 4)))
    w_down = bell_draw(keys[3], (FF, D), (FF // 2) ** -0.5, 0.046875, ((0, 4), (1, 4)))
    block_mask = place_ends((jax.random.randint(keys[4], (NFB, NDB), 0, 2) < 1).astype(jnp.int32), jax.random.fold_in(keys[4], 1), 0, 1)
    return dict(grad_out=grad_out, gate_pre=gate_pre, up_pre=up_pre, w_down=w_down, block_mask=block_mask)


def reference(grad_out, gate_pre, up_pre, w_down, block_mask):
    keep = jnp.repeat(jnp.repeat(block_mask > 0, BLOCK, axis=0), BLOCK, axis=1)
    w_kept = jnp.where(keep, w_down, jnp.zeros_like(w_down))
    gate = gate_pre.astype(jnp.float32)
    up = up_pre.astype(jnp.float32)
    sig = jax.nn.sigmoid(gate)
    act = (gate * sig * up).astype(jnp.bfloat16)
    flat = grad_out.reshape(N_DP * GROUP, D)
    width = D // N_COL

    def add_slice(k, total):
        start = (k * width).astype(jnp.int32)
        piece = lax.dynamic_slice_in_dim(flat, start, width, 1)
        weights = lax.dynamic_slice_in_dim(w_kept, start, width, 1)
        term = lax.dot_general(piece, weights, (((1,), (1,)), ((), ())), preferred_element_type=jnp.float32)
        term = lax.optimization_barrier(term.astype(jnp.bfloat16))
        return total + term.astype(jnp.float32)
    dact = lax.fori_loop(jnp.int32(0), jnp.int32(N_COL), add_slice, jnp.zeros((N_DP * GROUP, FF), jnp.float32))
    dact = dact.reshape(N_DP, GROUP, FF)
    grad_gate = (dact * up * sig * (1.0 + gate * (1.0 - sig))).astype(jnp.bfloat16)
    grad_up = (dact * gate * sig).astype(jnp.bfloat16)
    act_flat = act.reshape(N_DP * GROUP, FF)
    total = lax.dot_general(act_flat, flat, (((0,), (0,)), ((), ())), preferred_element_type=jnp.float32)
    scale = 1.0 / jnp.sqrt(jnp.float32(N_DP * GROUP))
    grad_down = jnp.where(keep, total * scale, jnp.zeros_like(total)).astype(jnp.bfloat16)
    return (grad_gate, grad_up, grad_down)
```

```python
import functools

import jax
import jax.numpy as jnp
from jax import lax
from jax.experimental import pallas as pl
from jax.experimental.pallas import tpu as pltpu
from jax.sharding import PartitionSpec as P

BLOCK = 128
ACT_CHUNKS = 2
SUM_CHUNKS = 2
VMEM_LIMIT = 40 * 1024 * 1024
bf16 = jnp.bfloat16
f32 = jnp.float32


def tile_of(size, largest):
    tile = largest
    while size % tile:
        tile //= 2
    return tile


def swap(x, axis, bit):
    n = lax.axis_size(axis)
    return lax.ppermute(x, axis, [(i, i ^ bit) for i in range(n)])


def masked_rows(w, mask_rows):
    parts = [
        w[k * BLOCK : (k + 1) * BLOCK, :] * m.astype(bf16) for k, m in enumerate(mask_rows)
    ]
    return parts[0] if len(parts) == 1 else jnp.concatenate(parts, axis=0)


def partial_kernel(base, place_ref, g0, g1, g2, g3, mask_ref, w_ref, stay_ref, next_ref, send_ref, lhs):
    step = pl.program_id(0)
    rows = g0.shape[0]

    @pl.when(step == 0)
    def _():
        for s, g in enumerate((g0, g1, g2, g3)):
            at = pl.multiple_of(place_ref[s] * rows, rows)
            lhs[pl.ds(at, rows), :] = g[...]

    tile = w_ref.shape[0]
    sub = min(tile, 256)
    for k in range(tile // sub):
        block = base + step * (tile // BLOCK) + k * (sub // BLOCK)
        masks = [mask_ref[pl.ds(block + j, 1), :] for j in range(sub // BLOCK)]
        w = masked_rows(w_ref[k * sub : (k + 1) * sub, :], masks)
        out = lax.dot_general(
            lhs[...], w, (((1,), (1,)), ((), ())), preferred_element_type=f32
        ).astype(bf16)
        at = slice(k * sub, (k + 1) * sub)
        stay_ref[:, at] = out[:rows]
        next_ref[:, at] = out[rows : 2 * rows]
        send_ref[:, at] = out[2 * rows :]


def partial_sums(place, grads, mask_rows, w, start, width):
    f_local, d_local = w.shape
    rows = grads[0].shape[0]
    tile = tile_of(width, 512)
    base = start // BLOCK
    whole = pl.BlockSpec((rows, d_local), lambda i, p: (0, 0))
    return pl.pallas_call(
        functools.partial(partial_kernel, base),
        grid_spec=pltpu.PrefetchScalarGridSpec(
            num_scalar_prefetch=1,
            grid=(width // tile,),
            in_specs=[whole] * 4
            + [
                pl.BlockSpec(mask_rows.shape, lambda i, p: (0, 0)),
                pl.BlockSpec((tile, d_local), lambda i, p: (start // tile + i, 0)),
            ],
            out_specs=[
                pl.BlockSpec((rows, tile), lambda i, p: (0, i)),
                pl.BlockSpec((rows, tile), lambda i, p: (0, i)),
                pl.BlockSpec((2 * rows, tile), lambda i, p: (0, i)),
            ],
            scratch_shapes=[pltpu.VMEM((4 * rows, d_local), bf16)],
        ),
        out_shape=[
            jax.ShapeDtypeStruct((rows, width), bf16),
            jax.ShapeDtypeStruct((rows, width), bf16),
            jax.ShapeDtypeStruct((2 * rows, width), bf16),
        ],
        compiler_params=pltpu.CompilerParams(vmem_limit_bytes=VMEM_LIMIT),
        cost_estimate=pl.CostEstimate(
            flops=2 * 4 * rows * width * d_local, bytes_accessed=2 * width * d_local, transcendentals=0
        ),
        name="partial_sums",
    )(place, *grads, mask_rows, w)


def weight_kernel(base, aliased, place_ref, *refs):
    acts, grads = refs[:8], refs[8:16]
    mask_ref = refs[16]
    out_ref, lhs, rhs = refs[17 + aliased :]
    step = pl.program_id(0)
    rows = grads[0].shape[0]

    @pl.when(step == 0)
    def _():
        for s, g in enumerate(grads):
            at = pl.multiple_of(place_ref[s] * rows, rows)
            rhs[pl.ds(at, rows), :] = g[...]

    for s, a in enumerate(acts):
        lhs[s * rows : (s + 1) * rows, :] = a[...]
    tile, d_local = out_ref.shape
    total = lax.dot_general(
        lhs[...], rhs[...], (((0,), (0,)), ((), ())), preferred_element_type=f32
    )
    for k in range(tile // BLOCK):
        m = mask_ref[pl.ds(base + step * (tile // BLOCK) + k, 1), :]
        at = slice(k * BLOCK, (k + 1) * BLOCK)
        out_ref[at, :] = (total[at, :] * m).astype(bf16)


def weight_grad(place, acts, grads, mask_scaled, start, f_local, so_far):
    rows, width = acts[0].shape
    d_local = grads[0].shape[1]
    tile = tile_of(width, 512)
    aliased = 0 if so_far is None else 1
    in_specs = (
        [pl.BlockSpec((rows, tile), lambda i, p: (0, i))] * 8
        + [pl.BlockSpec((rows, d_local), lambda i, p: (0, 0))] * 8
        + [pl.BlockSpec(mask_scaled.shape, lambda i, p: (0, 0))]
        + [pl.BlockSpec(memory_space=pl.ANY)] * aliased
    )
    operands = (place, *acts, *grads, mask_scaled) + ((so_far,) if aliased else ())
    return pl.pallas_call(
        functools.partial(weight_kernel, start // BLOCK, aliased),
        grid_spec=pltpu.PrefetchScalarGridSpec(
            num_scalar_prefetch=1,
            grid=(width // tile,),
            in_specs=in_specs,
            out_specs=pl.BlockSpec((tile, d_local), lambda i, p: (start // tile + i, 0)),
            scratch_shapes=[
                pltpu.VMEM((8 * rows, tile), bf16),
                pltpu.VMEM((8 * rows, d_local), bf16),
            ],
        ),
        out_shape=jax.ShapeDtypeStruct((f_local, d_local), bf16),
        input_output_aliases={18: 0} if aliased else {},
        compiler_params=pltpu.CompilerParams(vmem_limit_bytes=VMEM_LIMIT),
        cost_estimate=pl.CostEstimate(
            flops=2 * 8 * rows * width * d_local, bytes_accessed=2 * width * d_local, transcendentals=0
        ),
        name="weight_grad",
    )(*operands)


def activation(gate, up):
    gate, up = gate.astype(f32), up.astype(f32)
    return (gate * jax.nn.sigmoid(gate) * up).astype(bf16)


def local(grad_out, gate_pre, up_pre, w_down, block_mask):
    f_local, d_local = w_down.shape
    row, col = lax.axis_index("row"), lax.axis_index("col")
    scale = 1.0 / jnp.sqrt(f32(lax.axis_size("dp") * lax.axis_size("row") * grad_out.shape[1]))
    own_mask = lax.dynamic_slice(
        block_mask,
        (row * (f_local // BLOCK), col * (d_local // BLOCK)),
        (f_local // BLOCK, d_local // BLOCK),
    )
    keep = jnp.repeat((own_mask > 0).astype(f32), BLOCK, axis=1)
    keep_scaled = keep * scale

    own = grad_out[0]
    rows = own.shape[0]
    grads = [own] + [swap(own, "row", s) for s in (1, 2, 3)]
    across = swap(own, "dp", 1)

    gate, up = gate_pre[0], up_pre[0]
    width = f_local // ACT_CHUNKS
    act_pieces = []
    for j in range(ACT_CHUNKS):
        at = slice(j * width, (j + 1) * width)
        a = activation(gate[:, at], up[:, at])
        a_y = swap(a, "col", 2)
        a_x = swap(a, "dp", 1)
        a_xy = swap(a_y, "dp", 1)
        act_pieces.append(
            [
                a, swap(a, "col", 1), a_y, swap(a_y, "col", 1),
                a_x, swap(a_x, "col", 1), a_xy, swap(a_xy, "col", 1),
            ]
        )
    others = [across] + [swap(across, "row", s) for s in (1, 2, 3)]

    away = jnp.stack([row ^ col ^ s for s in range(4)]).astype(jnp.int32)
    by_dest = jnp.array([0, 2, 1, 3], jnp.int32)[away]
    by_act = jnp.concatenate([away, away + 4])

    span = f_local // SUM_CHUNKS
    sums = []
    for j in range(SUM_CHUNKS):
        stay, onward, send = partial_sums(by_dest, grads, keep, w_down, j * span, span)
        got = swap(send, "col", 1)
        mine = stay.astype(f32) + got[:rows].astype(f32)
        theirs = (onward.astype(f32) + got[rows:].astype(f32)).astype(bf16)
        sums.append((mine, swap(theirs, "col", 2)))

    grad_down = None
    for j in range(ACT_CHUNKS):
        grad_down = weight_grad(
            by_act, act_pieces[j], grads + others, keep_scaled, j * width, f_local, grad_down
        )

    gg, gu = [], []
    for j, (mine, got) in enumerate(sums):
        at = slice(j * span, (j + 1) * span)
        dact = mine + got.astype(f32)
        g, u = gate[:, at].astype(f32), up[:, at].astype(f32)
        sig = jax.nn.sigmoid(g)
        gg.append((dact * u * sig * (1.0 + g * (1.0 - sig))).astype(bf16))
        gu.append((dact * g * sig).astype(bf16))
    return (
        jnp.concatenate(gg, axis=1)[None],
        jnp.concatenate(gu, axis=1)[None],
        grad_down,
    )


def general(grad_out, gate_pre, up_pre, w_down, block_mask):
    f_local, d_local = w_down.shape
    row_block = (lax.axis_index("row") * f_local + jnp.arange(f_local)) // BLOCK
    col_block = (lax.axis_index("col") * d_local + jnp.arange(d_local)) // BLOCK
    keep = block_mask[row_block][:, col_block] > 0
    w_kept = jnp.where(keep, w_down, jnp.zeros_like(w_down))
    gate, up = gate_pre[0].astype(f32), up_pre[0].astype(f32)
    sig = jax.nn.sigmoid(gate)
    act = (gate * sig * up).astype(bf16)
    grads = lax.all_gather(grad_out[0], "row", axis=0, tiled=True)
    partial = lax.dot_general(
        grads, w_kept, (((1,), (1,)), ((), ())), preferred_element_type=f32
    ).astype(bf16)
    dact = lax.psum_scatter(partial, "col", scatter_dimension=0, tiled=True).astype(f32)
    acts = lax.all_gather(act, ("dp", "col"), axis=0, tiled=True)
    every = lax.all_gather(grads, "dp", axis=0, tiled=True)
    total = lax.dot_general(acts, every, (((0,), (0,)), ((), ())), preferred_element_type=f32)
    scale = 1.0 / jnp.sqrt(f32(every.shape[0]))
    grad_down = jnp.where(keep, total * scale, jnp.zeros_like(total)).astype(bf16)
    grad_gate = (dact * up * sig * (1.0 + gate * (1.0 - sig))).astype(bf16)
    grad_up = (dact * gate * sig).astype(bf16)
    return grad_gate[None], grad_up[None], grad_down


def solution(mesh):
    placed = (
        P("dp", "row", "col"),
        P("dp", "col", "row"),
        P("dp", "col", "row"),
        P("row", "col"),
        P(),
    )
    size = dict(mesh.shape)
    pairwise = size["row"] == 4 and size["col"] == 4 and size["dp"] == 2

    def run(grad_out, gate_pre, up_pre, w_down, block_mask):
        f_local, d_local = w_down.shape
        rows = grad_out.shape[1]
        fits = pairwise and rows == gate_pre.shape[1] and rows % 16 == 0
        for chunks in (ACT_CHUNKS, SUM_CHUNKS):
            fits = fits and f_local % (chunks * BLOCK) == 0
        fits = fits and d_local % BLOCK == 0
        step = local if fits else general
        return step(grad_out, gate_pre, up_pre, w_down, block_mask)

    return jax.shard_map(
        run,
        mesh=mesh,
        in_specs=placed,
        out_specs=(P("dp", "col", "row"), P("dp", "col", "row"), P("row", "col")),
        check_vma=False,
    )
```

```python
import jax
import jax.numpy as jnp
from jax import lax
from jax.experimental import pallas as pl
from jax.experimental.pallas import tpu as pltpu
from jax.sharding import PartitionSpec as P

BLOCK = 128
SUB = 256
IN_TILE = 512
HEAD = 8
TAIL = (4, 4)
OUT_TILE = 256
SMALL_VMEM = 4 * 1024 * 1024
PARTIAL_VMEM = 24 * 1024 * 1024
WEIGHT_VMEM = 48 * 1024 * 1024
bf16 = jnp.bfloat16
f32 = jnp.float32


def swap(x, axis, bit):
    n = lax.axis_size(axis)
    return lax.ppermute(x, axis, [(i, i ^ bit) for i in range(n)])


def dest_slot(v):
    return (v >> 1) | ((v & 1) << 1)


def stack_kernel(pos_ref, g0, g1, g2, g3, out_ref):
    rows = g0.shape[0]
    for s, g in enumerate((g0, g1, g2, g3)):
        at = pl.multiple_of(dest_slot(pos_ref[0] ^ s) * rows, rows)
        out_ref[pl.ds(at, rows), :] = g[...]


def stack(pos, grads):
    rows, d_local = grads[0].shape
    vmem = pl.BlockSpec(memory_space=pltpu.VMEM)
    return pl.pallas_call(
        stack_kernel,
        in_specs=[pl.BlockSpec(memory_space=pltpu.SMEM)] + [vmem] * 4,
        out_specs=vmem,
        out_shape=jax.ShapeDtypeStruct((4 * rows, d_local), bf16),
        compiler_params=pltpu.CompilerParams(vmem_limit_bytes=SMALL_VMEM),
        name="stack_tokens",
    )(pos, *grads)


def fetch_kernel(w_ref, held_ref, done_ref, sems):
    def enter(i):
        at = pl.ds(i * IN_TILE, IN_TILE)
        return pltpu.make_async_copy(w_ref.at[at, :], held_ref.at[at, :], sems.at[i])

    tiles = held_ref.shape[0] // IN_TILE
    for i in range(tiles):
        enter(i).start()
    done_ref[...] = jnp.zeros_like(done_ref)
    for i in range(tiles):
        enter(i).wait()


def fetch(w):
    rows = w.shape[0] // IN_TILE * HEAD // 16 * IN_TILE
    anywhere = pl.BlockSpec(memory_space=pl.ANY)
    return pl.pallas_call(
        fetch_kernel,
        in_specs=[anywhere],
        out_specs=[anywhere, pl.BlockSpec(memory_space=pltpu.VMEM)],
        scratch_shapes=[pltpu.SemaphoreType.DMA((rows // IN_TILE,))],
        out_shape=[pltpu.VMEM((rows, w.shape[1]), bf16), jax.ShapeDtypeStruct((8, BLOCK), f32)],
        compiler_params=pltpu.CompilerParams(vmem_limit_bytes=SMALL_VMEM),
        cost_estimate=pl.CostEstimate(flops=0, bytes_accessed=2 * rows * w.shape[1], transcendentals=0),
        name="fetch_weights",
    )(pltpu.with_memory_space_constraint(w, pltpu.HBM))


def partial_kernel(lhs, mask_ref, head_ref, _, w_ref, stay_ref, next_ref, send_ref, held, sems):
    rows = stay_ref.shape[0]
    first = head_ref.shape[0]
    ends = []
    for t in TAIL:
        ends.append((ends[-1] if ends else first) + w_ref.shape[0] // 16 * t)

    def enter(i):
        start = ends[i - 1] if i else first
        return pltpu.make_async_copy(
            w_ref.at[pl.ds(start, ends[i] - start), :],
            held.at[pl.ds(start - first, ends[i] - start), :],
            sems.at[i],
        )

    for i in range(len(ends)):
        enter(i).start()
    for k in range(w_ref.shape[0] // SUB):
        parts = []
        for j in range(SUB // BLOCK):
            r = k * (SUB // BLOCK) + j
            if r * BLOCK < first:
                w = head_ref[r * BLOCK : (r + 1) * BLOCK, :]
            else:
                if r * BLOCK in [first] + ends[:-1]:
                    enter(([first] + ends).index(r * BLOCK)).wait()
                w = held[r * BLOCK - first : (r + 1) * BLOCK - first, :]
            parts.append(w * mask_ref[r : r + 1, :].astype(bf16))
        out = lax.dot_general(
            jnp.concatenate(parts, axis=0),
            lhs[...],
            (((1,), (1,)), ((), ())),
            preferred_element_type=f32,
        ).T.astype(bf16)
        at = slice(k * SUB, (k + 1) * SUB)
        stay_ref[:, at] = out[:rows]
        next_ref[:, at] = out[rows : 2 * rows]
        send_ref[:, at] = out[2 * rows :]


def partial_sums(tokens, mask_rows, head, mark, w):
    f_local, d_local = w.shape
    rows = tokens.shape[0] // 4
    vmem = pl.BlockSpec(memory_space=pltpu.VMEM)
    return pl.pallas_call(
        partial_kernel,
        in_specs=[vmem] * 3 + [pl.BlockSpec(memory_space=pl.ANY)] * 2,
        out_specs=[vmem] * 3,
        scratch_shapes=[
            pltpu.VMEM((f_local - head.shape[0], d_local), bf16),
            pltpu.SemaphoreType.DMA((len(TAIL),)),
        ],
        out_shape=[
            jax.ShapeDtypeStruct((rows, f_local), bf16),
            jax.ShapeDtypeStruct((rows, f_local), bf16),
            jax.ShapeDtypeStruct((2 * rows, f_local), bf16),
        ],
        compiler_params=pltpu.CompilerParams(vmem_limit_bytes=PARTIAL_VMEM),
        cost_estimate=pl.CostEstimate(
            flops=2 * 4 * rows * f_local * d_local, bytes_accessed=2 * f_local * d_local, transcendentals=0
        ),
        name="partial_sums",
    )(
        tokens,
        mask_rows,
        pltpu.with_memory_space_constraint(head, pltpu.VMEM),
        mark,
        pltpu.with_memory_space_constraint(w, pltpu.HBM),
    )


def weight_kernel(*refs):
    acts, tokens = refs[:8], refs[8:10]
    mask_ref, out_ref, held, sems = refs[10:]
    f_local = acts[0].shape[1]
    tiles = f_local // OUT_TILE

    def leave(i):
        return pltpu.make_async_copy(
            held.at[i], out_ref.at[pl.ds(i * OUT_TILE, OUT_TILE), :], sems.at[i]
        )

    rhs = jnp.concatenate([t[...] for t in tokens], axis=0)
    for i in range(tiles):
        at = slice(i * OUT_TILE, (i + 1) * OUT_TILE)
        lhs = jnp.concatenate([a[:, at] for a in acts], axis=0)
        total = lax.dot_general(lhs, rhs, (((0,), (0,)), ((), ())), preferred_element_type=f32)
        for k in range(OUT_TILE // BLOCK):
            r = i * (OUT_TILE // BLOCK) + k
            part = slice(k * BLOCK, (k + 1) * BLOCK)
            held[i, part, :] = (total[part, :] * mask_ref[r : r + 1, :]).astype(bf16)
        leave(i).start()
    for i in range(tiles):
        leave(i).wait()


def weight_grad(acts, tokens, mask_scaled):
    f_local = acts[0].shape[1]
    every, d_local = 2 * tokens[0].shape[0], tokens[0].shape[1]
    vmem = pl.BlockSpec(memory_space=pltpu.VMEM)
    tiles = f_local // OUT_TILE
    return pl.pallas_call(
        weight_kernel,
        in_specs=[vmem] * 11,
        out_specs=pl.BlockSpec(memory_space=pl.ANY),
        scratch_shapes=[
            pltpu.VMEM((tiles, OUT_TILE, d_local), bf16),
            pltpu.SemaphoreType.DMA((tiles,)),
        ],
        out_shape=jax.ShapeDtypeStruct((f_local, d_local), bf16),
        compiler_params=pltpu.CompilerParams(vmem_limit_bytes=WEIGHT_VMEM),
        cost_estimate=pl.CostEstimate(
            flops=2 * every * f_local * d_local, bytes_accessed=2 * f_local * d_local, transcendentals=0
        ),
        name="weight_grad",
    )(*acts, *tokens, mask_scaled)


def activation(gate, up):
    gate, up = gate.astype(f32), up.astype(f32)
    return (gate * jax.nn.sigmoid(gate) * up).astype(bf16)


def local(grad_out, gate_pre, up_pre, w_down, block_mask):
    f_local, d_local = w_down.shape
    row, col = lax.axis_index("row"), lax.axis_index("col")
    scale = 1.0 / jnp.sqrt(f32(lax.axis_size("dp") * lax.axis_size("row") * grad_out.shape[1]))
    own_mask = lax.dynamic_slice(
        block_mask,
        (row * (f_local // BLOCK), col * (d_local // BLOCK)),
        (f_local // BLOCK, d_local // BLOCK),
    )
    keep = jnp.repeat((own_mask > 0).astype(f32), BLOCK, axis=1)
    keep_scaled = keep * scale

    gate, up = gate_pre[0], up_pre[0]
    own = grad_out[0]
    rows = own.shape[0]

    grads = [own] + [swap(own, "row", s) for s in (1, 2, 3)]
    act = activation(gate, up)
    act_x, act_y = swap(act, "dp", 1), swap(act, "col", 2)

    pos = jnp.full((1,), row ^ col, jnp.int32)
    tokens = stack(pos, grads)
    head, mark = fetch(w_down)
    act_c = swap(act, "col", 1)
    tokens, act, act_c, act_x, act_y, keep, keep_scaled, mark = lax.optimization_barrier(
        (tokens, act, act_c, act_x, act_y, keep, keep_scaled, mark)
    )

    tokens_x, act_xy = swap(tokens, "dp", 1), swap(act_x, "col", 2)
    stay, onward, send = partial_sums(tokens, keep, head, mark, w_down)
    send, tokens_x, act_xy = lax.optimization_barrier((send, tokens_x, act_xy))

    got = swap(send, "col", 1)
    act_yc, act_xc, act_xyc = [swap(a, "col", 1) for a in (act_y, act_x, act_xy)]
    mine = stay.astype(f32) + got[:rows].astype(f32)
    theirs = (onward.astype(f32) + got[rows:].astype(f32)).astype(bf16)
    last = swap(theirs, "col", 2)

    acts = [act, act_y, act_c, act_yc, act_x, act_xy, act_xc, act_xyc]
    grad_down = weight_grad(acts, [tokens, tokens_x], keep_scaled)

    dact = mine + last.astype(f32)
    gate, up = gate.astype(f32), up.astype(f32)
    sig = jax.nn.sigmoid(gate)
    grad_gate = (dact * up * sig * (1.0 + gate * (1.0 - sig))).astype(bf16)
    grad_up = (dact * gate * sig).astype(bf16)
    return grad_gate[None], grad_up[None], grad_down


def general(grad_out, gate_pre, up_pre, w_down, block_mask):
    f_local, d_local = w_down.shape
    row_block = (lax.axis_index("row") * f_local + jnp.arange(f_local)) // BLOCK
    col_block = (lax.axis_index("col") * d_local + jnp.arange(d_local)) // BLOCK
    keep = block_mask[row_block][:, col_block] > 0
    w_kept = jnp.where(keep, w_down, jnp.zeros_like(w_down))
    gate, up = gate_pre[0].astype(f32), up_pre[0].astype(f32)
    sig = jax.nn.sigmoid(gate)
    act = (gate * sig * up).astype(bf16)
    grads = lax.all_gather(grad_out[0], "row", axis=0, tiled=True)
    partial = lax.dot_general(
        grads, w_kept, (((1,), (1,)), ((), ())), preferred_element_type=f32
    ).astype(bf16)
    dact = lax.psum_scatter(partial, "col", scatter_dimension=0, tiled=True).astype(f32)
    acts = lax.all_gather(act, ("dp", "col"), axis=0, tiled=True)
    every = lax.all_gather(grads, "dp", axis=0, tiled=True)
    total = lax.dot_general(acts, every, (((0,), (0,)), ((), ())), preferred_element_type=f32)
    scale = 1.0 / jnp.sqrt(f32(every.shape[0]))
    grad_down = jnp.where(keep, total * scale, jnp.zeros_like(total)).astype(bf16)
    grad_gate = (dact * up * sig * (1.0 + gate * (1.0 - sig))).astype(bf16)
    grad_up = (dact * gate * sig).astype(bf16)
    return grad_gate[None], grad_up[None], grad_down


def solution(mesh):
    placed = (
        P("dp", "row", "col"),
        P("dp", "col", "row"),
        P("dp", "col", "row"),
        P("row", "col"),
        P(),
    )
    size = dict(mesh.shape)
    pairwise = size["row"] == 4 and size["col"] == 4 and size["dp"] == 2

    def run(grad_out, gate_pre, up_pre, w_down, block_mask):
        f_local, d_local = w_down.shape
        rows = grad_out.shape[1]
        fits = pairwise and rows == gate_pre.shape[1] and rows % 16 == 0
        fits = fits and f_local % 1024 == 0 and d_local % BLOCK == 0
        step = local if fits else general
        return step(grad_out, gate_pre, up_pre, w_down, block_mask)

    return jax.shard_map(
        run,
        mesh=mesh,
        in_specs=placed,
        out_specs=(P("dp", "col", "row"), P("dp", "col", "row"), P("row", "col")),
        check_vma=False,
    )
```

```python
import jax
import jax.numpy as jnp
from jax import lax
from jax.experimental import pallas as pl
from jax.experimental.pallas import tpu as pltpu
from jax.sharding import PartitionSpec as P

BLOCK = 128
SUB = 256
IN_TILE = 512
HEAD = 8
OUT_TILE = 256
SMALL_VMEM = 4 * 1024 * 1024
PARTIAL_VMEM = 24 * 1024 * 1024
WEIGHT_VMEM = 48 * 1024 * 1024
bf16 = jnp.bfloat16
f32 = jnp.float32


def swap(x, axis, bit):
    n = lax.axis_size(axis)
    return lax.ppermute(x, axis, [(i, i ^ bit) for i in range(n)])


def dest_slot(v):
    return (v >> 1) | ((v & 1) << 1)


def stack_kernel(pos_ref, g0, g1, g2, g3, out_ref):
    rows = g0.shape[0]
    for s, g in enumerate((g0, g1, g2, g3)):
        at = pl.multiple_of(dest_slot(pos_ref[0] ^ s) * rows, rows)
        out_ref[pl.ds(at, rows), :] = g[...]


def stack(pos, grads):
    rows, d_local = grads[0].shape
    vmem = pl.BlockSpec(memory_space=pltpu.VMEM)
    return pl.pallas_call(
        stack_kernel,
        in_specs=[pl.BlockSpec(memory_space=pltpu.SMEM)] + [vmem] * 4,
        out_specs=vmem,
        out_shape=jax.ShapeDtypeStruct((4 * rows, d_local), bf16),
        compiler_params=pltpu.CompilerParams(vmem_limit_bytes=SMALL_VMEM),
        name="stack_tokens",
    )(pos, *grads)


def fetch_kernel(w_ref, held_ref, done_ref, sems):
    def enter(i):
        at = pl.ds(i * IN_TILE, IN_TILE)
        return pltpu.make_async_copy(w_ref.at[at, :], held_ref.at[at, :], sems.at[i])

    tiles = held_ref.shape[0] // IN_TILE
    for i in range(tiles):
        enter(i).start()
    done_ref[...] = jnp.zeros_like(done_ref)
    for i in range(tiles):
        enter(i).wait()


def fetch(w):
    rows = w.shape[0] // IN_TILE * HEAD // 14 * IN_TILE
    anywhere = pl.BlockSpec(memory_space=pl.ANY)
    return pl.pallas_call(
        fetch_kernel,
        in_specs=[anywhere],
        out_specs=[anywhere, pl.BlockSpec(memory_space=pltpu.VMEM)],
        scratch_shapes=[pltpu.SemaphoreType.DMA((rows // IN_TILE,))],
        out_shape=[pltpu.VMEM((rows, w.shape[1]), bf16), jax.ShapeDtypeStruct((8, BLOCK), f32)],
        compiler_params=pltpu.CompilerParams(vmem_limit_bytes=SMALL_VMEM),
        cost_estimate=pl.CostEstimate(flops=0, bytes_accessed=2 * rows * w.shape[1], transcendentals=0),
        name="fetch_weights",
    )(pltpu.with_memory_space_constraint(w, pltpu.HBM))


def partial_kernel(lhs, mask_ref, head_ref, _, w_ref, stay_ref, next_ref, send_ref, held, sems):
    rows = stay_ref.shape[0]
    first = head_ref.shape[0]
    ends = [first + (w_ref.shape[0] - first) // 2, w_ref.shape[0]]

    def enter(i):
        start = ends[i - 1] if i else first
        return pltpu.make_async_copy(
            w_ref.at[pl.ds(start, ends[i] - start), :],
            held.at[pl.ds(start - first, ends[i] - start), :],
            sems.at[i],
        )

    for i in range(len(ends)):
        enter(i).start()
    for k in range(w_ref.shape[0] // SUB):
        parts = []
        for j in range(SUB // BLOCK):
            r = k * (SUB // BLOCK) + j
            if r * BLOCK < first:
                w = head_ref[r * BLOCK : (r + 1) * BLOCK, :]
            else:
                if r * BLOCK in [first] + ends[:-1]:
                    enter(([first] + ends).index(r * BLOCK)).wait()
                w = held[r * BLOCK - first : (r + 1) * BLOCK - first, :]
            parts.append(w * mask_ref[r : r + 1, :].astype(bf16))
        out = lax.dot_general(
            jnp.concatenate(parts, axis=0),
            lhs[...],
            (((1,), (1,)), ((), ())),
            preferred_element_type=f32,
        ).T.astype(bf16)
        at = slice(k * SUB, (k + 1) * SUB)
        stay_ref[:, at] = out[:rows]
        next_ref[:, at] = out[rows : 2 * rows]
        send_ref[:, at] = out[2 * rows :]


def partial_sums(tokens, mask_rows, head, mark, w):
    f_local, d_local = w.shape
    rows = tokens.shape[0] // 4
    vmem = pl.BlockSpec(memory_space=pltpu.VMEM)
    return pl.pallas_call(
        partial_kernel,
        in_specs=[vmem] * 3 + [pl.BlockSpec(memory_space=pl.ANY)] * 2,
        out_specs=[vmem] * 3,
        scratch_shapes=[
            pltpu.VMEM((f_local - head.shape[0], d_local), bf16),
            pltpu.SemaphoreType.DMA((2,)),
        ],
        out_shape=[
            jax.ShapeDtypeStruct((rows, f_local), bf16),
            jax.ShapeDtypeStruct((rows, f_local), bf16),
            jax.ShapeDtypeStruct((2 * rows, f_local), bf16),
        ],
        compiler_params=pltpu.CompilerParams(vmem_limit_bytes=PARTIAL_VMEM),
        cost_estimate=pl.CostEstimate(
            flops=2 * 4 * rows * f_local * d_local, bytes_accessed=2 * f_local * d_local, transcendentals=0
        ),
        name="partial_sums",
    )(
        tokens,
        mask_rows,
        pltpu.with_memory_space_constraint(head, pltpu.VMEM),
        mark,
        pltpu.with_memory_space_constraint(w, pltpu.HBM),
    )


def weight_kernel(*refs):
    acts, tokens = refs[:8], refs[8:10]
    mask_ref, out_ref, held, sems = refs[10:]
    f_local = acts[0].shape[1]
    tiles = f_local // OUT_TILE

    def leave(i):
        return pltpu.make_async_copy(
            held.at[i], out_ref.at[pl.ds(i * OUT_TILE, OUT_TILE), :], sems.at[i]
        )

    rhs = jnp.concatenate([t[...] for t in tokens], axis=0)
    for i in range(tiles):
        at = slice(i * OUT_TILE, (i + 1) * OUT_TILE)
        lhs = jnp.concatenate([a[:, at] for a in acts], axis=0)
        total = lax.dot_general(lhs, rhs, (((0,), (0,)), ((), ())), preferred_element_type=f32)
        for k in range(OUT_TILE // BLOCK):
            r = i * (OUT_TILE // BLOCK) + k
            part = slice(k * BLOCK, (k + 1) * BLOCK)
            held[i, part, :] = (total[part, :] * mask_ref[r : r + 1, :]).astype(bf16)
        leave(i).start()
    for i in range(tiles):
        leave(i).wait()


def weight_grad(acts, tokens, mask_scaled):
    f_local = acts[0].shape[1]
    every, d_local = 2 * tokens[0].shape[0], tokens[0].shape[1]
    vmem = pl.BlockSpec(memory_space=pltpu.VMEM)
    tiles = f_local // OUT_TILE
    return pl.pallas_call(
        weight_kernel,
        in_specs=[vmem] * 11,
        out_specs=pl.BlockSpec(memory_space=pl.ANY),
        scratch_shapes=[
            pltpu.VMEM((tiles, OUT_TILE, d_local), bf16),
            pltpu.SemaphoreType.DMA((tiles,)),
        ],
        out_shape=jax.ShapeDtypeStruct((f_local, d_local), bf16),
        compiler_params=pltpu.CompilerParams(vmem_limit_bytes=WEIGHT_VMEM),
        cost_estimate=pl.CostEstimate(
            flops=2 * every * f_local * d_local, bytes_accessed=2 * f_local * d_local, transcendentals=0
        ),
        name="weight_grad",
    )(*acts, *tokens, mask_scaled)


def activation(gate, up):
    gate, up = gate.astype(f32), up.astype(f32)
    return (gate * jax.nn.sigmoid(gate) * up).astype(bf16)


def local(grad_out, gate_pre, up_pre, w_down, block_mask):
    f_local, d_local = w_down.shape
    row, col = lax.axis_index("row"), lax.axis_index("col")
    scale = 1.0 / jnp.sqrt(f32(lax.axis_size("dp") * lax.axis_size("row") * grad_out.shape[1]))
    own_mask = lax.dynamic_slice(
        block_mask,
        (row * (f_local // BLOCK), col * (d_local // BLOCK)),
        (f_local // BLOCK, d_local // BLOCK),
    )
    keep = jnp.repeat((own_mask > 0).astype(f32), BLOCK, axis=1)
    keep_scaled = keep * scale

    gate, up = gate_pre[0], up_pre[0]
    own = grad_out[0]
    rows = own.shape[0]

    grads = [own] + [swap(own, "row", s) for s in (1, 2, 3)]
    act = activation(gate, up)
    act_x, act_y = swap(act, "dp", 1), swap(act, "col", 2)

    pos = jnp.full((1,), row ^ col, jnp.int32)
    tokens = stack(pos, grads)
    head, mark = fetch(w_down)
    tokens, keep, keep_scaled, mark = lax.optimization_barrier(
        (tokens, keep, keep_scaled, mark)
    )

    tokens_x, act_xy = swap(tokens, "dp", 1), swap(act_x, "col", 2)
    tokens, act, act_y, act_x, keep, mark = lax.optimization_barrier(
        (tokens, act, act_y, act_x, keep, mark)
    )
    stay, onward, send = partial_sums(tokens, keep, head, mark, w_down)
    send, tokens_x, act_xy = lax.optimization_barrier((send, tokens_x, act_xy))

    got = swap(send, "col", 1)
    act_c, act_yc, act_xc, act_xyc = [swap(a, "col", 1) for a in (act, act_y, act_x, act_xy)]
    mine = stay.astype(f32) + got[:rows].astype(f32)
    theirs = (onward.astype(f32) + got[rows:].astype(f32)).astype(bf16)
    last = swap(theirs, "col", 2)

    acts = [act, act_y, act_c, act_yc, act_x, act_xy, act_xc, act_xyc]
    grad_down = weight_grad(acts, [tokens, tokens_x], keep_scaled)

    dact = mine + last.astype(f32)
    gate, up = gate.astype(f32), up.astype(f32)
    sig = jax.nn.sigmoid(gate)
    grad_gate = (dact * up * sig * (1.0 + gate * (1.0 - sig))).astype(bf16)
    grad_up = (dact * gate * sig).astype(bf16)
    return grad_gate[None], grad_up[None], grad_down


def general(grad_out, gate_pre, up_pre, w_down, block_mask):
    f_local, d_local = w_down.shape
    row_block = (lax.axis_index("row") * f_local + jnp.arange(f_local)) // BLOCK
    col_block = (lax.axis_index("col") * d_local + jnp.arange(d_local)) // BLOCK
    keep = block_mask[row_block][:, col_block] > 0
    w_kept = jnp.where(keep, w_down, jnp.zeros_like(w_down))
    gate, up = gate_pre[0].astype(f32), up_pre[0].astype(f32)
    sig = jax.nn.sigmoid(gate)
    act = (gate * sig * up).astype(bf16)
    grads = lax.all_gather(grad_out[0], "row", axis=0, tiled=True)
    partial = lax.dot_general(
        grads, w_kept, (((1,), (1,)), ((), ())), preferred_element_type=f32
    ).astype(bf16)
    dact = lax.psum_scatter(partial, "col", scatter_dimension=0, tiled=True).astype(f32)
    acts = lax.all_gather(act, ("dp", "col"), axis=0, tiled=True)
    every = lax.all_gather(grads, "dp", axis=0, tiled=True)
    total = lax.dot_general(acts, every, (((0,), (0,)), ((), ())), preferred_element_type=f32)
    scale = 1.0 / jnp.sqrt(f32(every.shape[0]))
    grad_down = jnp.where(keep, total * scale, jnp.zeros_like(total)).astype(bf16)
    grad_gate = (dact * up * sig * (1.0 + gate * (1.0 - sig))).astype(bf16)
    grad_up = (dact * gate * sig).astype(bf16)
    return grad_gate[None], grad_up[None], grad_down


def solution(mesh):
    placed = (
        P("dp", "row", "col"),
        P("dp", "col", "row"),
        P("dp", "col", "row"),
        P("row", "col"),
        P(),
    )
    size = dict(mesh.shape)
    pairwise = size["row"] == 4 and size["col"] == 4 and size["dp"] == 2

    def run(grad_out, gate_pre, up_pre, w_down, block_mask):
        f_local, d_local = w_down.shape
        rows = grad_out.shape[1]
        fits = pairwise and rows == gate_pre.shape[1] and rows % 16 == 0
        fits = fits and f_local % 1024 == 0 and d_local % BLOCK == 0
        step = local if fits else general
        return step(grad_out, gate_pre, up_pre, w_down, block_mask)

    return jax.shard_map(
        run,
        mesh=mesh,
        in_specs=placed,
        out_specs=(P("dp", "col", "row"), P("dp", "col", "row"), P("row", "col")),
        check_vma=False,
    )
```

```python
import jax
import jax.numpy as jnp
from jax import lax
from jax.experimental import pallas as pl
from jax.experimental.pallas import tpu as pltpu
from jax.sharding import PartitionSpec as P

BLOCK = 128
SUB = 256
IN_TILE = 512
TAIL_STEPS = 4
HEAD = 8
OUT_TILE = 256
SMALL_VMEM = 4 * 1024 * 1024
PARTIAL_VMEM = 24 * 1024 * 1024
WEIGHT_VMEM = 48 * 1024 * 1024
bf16 = jnp.bfloat16
f32 = jnp.float32


def swap(x, axis, bit):
    n = lax.axis_size(axis)
    return lax.ppermute(x, axis, [(i, i ^ bit) for i in range(n)])


def dest_slot(v):
    return (v >> 1) | ((v & 1) << 1)


def stack_kernel(pos_ref, g0, g1, g2, g3, out_ref):
    rows = g0.shape[0]
    for s, g in enumerate((g0, g1, g2, g3)):
        at = pl.multiple_of(dest_slot(pos_ref[0] ^ s) * rows, rows)
        out_ref[pl.ds(at, rows), :] = g[...]


def stack(pos, grads):
    rows, d_local = grads[0].shape
    vmem = pl.BlockSpec(memory_space=pltpu.VMEM)
    return pl.pallas_call(
        stack_kernel,
        in_specs=[pl.BlockSpec(memory_space=pltpu.SMEM)] + [vmem] * 4,
        out_specs=vmem,
        out_shape=jax.ShapeDtypeStruct((4 * rows, d_local), bf16),
        compiler_params=pltpu.CompilerParams(vmem_limit_bytes=SMALL_VMEM),
        name="stack_tokens",
    )(pos, *grads)


def fetch_kernel(w_ref, held_ref, done_ref, sems):
    def enter(i):
        at = pl.ds(i * IN_TILE, IN_TILE)
        return pltpu.make_async_copy(w_ref.at[at, :], held_ref.at[at, :], sems.at[i])

    tiles = held_ref.shape[0] // IN_TILE
    for i in range(tiles):
        enter(i).start()
    done_ref[...] = jnp.zeros_like(done_ref)
    for i in range(tiles):
        enter(i).wait()


def fetch(w):
    rows = w.shape[0] // IN_TILE * HEAD // 14 * IN_TILE
    anywhere = pl.BlockSpec(memory_space=pl.ANY)
    return pl.pallas_call(
        fetch_kernel,
        in_specs=[anywhere],
        out_specs=[anywhere, pl.BlockSpec(memory_space=pltpu.VMEM)],
        scratch_shapes=[pltpu.SemaphoreType.DMA((rows // IN_TILE,))],
        out_shape=[pltpu.VMEM((rows, w.shape[1]), bf16), jax.ShapeDtypeStruct((8, BLOCK), f32)],
        compiler_params=pltpu.CompilerParams(vmem_limit_bytes=SMALL_VMEM),
        cost_estimate=pl.CostEstimate(flops=0, bytes_accessed=2 * rows * w.shape[1], transcendentals=0),
        name="fetch_weights",
    )(pltpu.with_memory_space_constraint(w, pltpu.HBM))


def partial_kernel(lhs, mask_ref, head_ref, _, w_ref, stay_ref, next_ref, send_ref, send_next_ref, held, sems):
    rows = stay_ref.shape[0]
    first = head_ref.shape[0]
    ends = [first + (w_ref.shape[0] - first) // 2, w_ref.shape[0]]

    def enter(i):
        start = ends[i - 1] if i else first
        return pltpu.make_async_copy(
            w_ref.at[pl.ds(start, ends[i] - start), :],
            held.at[pl.ds(start - first, ends[i] - start), :],
            sems.at[i],
        )

    for i in range(len(ends)):
        enter(i).start()
    for k in range(w_ref.shape[0] // SUB):
        parts = []
        for j in range(SUB // BLOCK):
            r = k * (SUB // BLOCK) + j
            if r * BLOCK < first:
                w = head_ref[r * BLOCK : (r + 1) * BLOCK, :]
            else:
                if r * BLOCK in [first] + ends[:-1]:
                    enter(([first] + ends).index(r * BLOCK)).wait()
                w = held[r * BLOCK - first : (r + 1) * BLOCK - first, :]
            parts.append(w * mask_ref[r : r + 1, :].astype(bf16))
        out = lax.dot_general(
            jnp.concatenate(parts, axis=0),
            lhs[...],
            (((1,), (1,)), ((), ())),
            preferred_element_type=f32,
        ).T.astype(bf16)
        at = slice(k * SUB, (k + 1) * SUB)
        stay_ref[:, at] = out[:rows]
        next_ref[:, at] = out[rows : 2 * rows]
        send_ref[:, at] = out[2 * rows : 3 * rows]
        send_next_ref[:, at] = out[3 * rows :]


def partial_sums(tokens, mask_rows, head, mark, w):
    f_local, d_local = w.shape
    rows = tokens.shape[0] // 4
    vmem = pl.BlockSpec(memory_space=pltpu.VMEM)
    return pl.pallas_call(
        partial_kernel,
        in_specs=[vmem] * 3 + [pl.BlockSpec(memory_space=pl.ANY)] * 2,
        out_specs=[vmem] * 4,
        scratch_shapes=[
            pltpu.VMEM((f_local - head.shape[0], d_local), bf16),
            pltpu.SemaphoreType.DMA((2,)),
        ],
        out_shape=[
            jax.ShapeDtypeStruct((rows, f_local), bf16),
        ]
        * 4,
        compiler_params=pltpu.CompilerParams(vmem_limit_bytes=PARTIAL_VMEM),
        cost_estimate=pl.CostEstimate(
            flops=2 * 4 * rows * f_local * d_local, bytes_accessed=2 * f_local * d_local, transcendentals=0
        ),
        name="partial_sums",
    )(
        tokens,
        mask_rows,
        pltpu.with_memory_space_constraint(head, pltpu.VMEM),
        mark,
        pltpu.with_memory_space_constraint(w, pltpu.HBM),
    )


def weight_kernel(*refs):
    acts, tokens = refs[:8], refs[8:10]
    mask_ref, out_ref, held, sems = refs[10:]
    f_local = acts[0].shape[1]
    tiles = f_local // OUT_TILE

    def leave(i):
        return pltpu.make_async_copy(
            held.at[i], out_ref.at[pl.ds(i * OUT_TILE, OUT_TILE), :], sems.at[i]
        )

    rhs = jnp.concatenate([t[...] for t in tokens], axis=0)
    for i in range(tiles):
        at = slice(i * OUT_TILE, (i + 1) * OUT_TILE)
        lhs = jnp.concatenate([a[:, at] for a in acts], axis=0)
        total = lax.dot_general(lhs, rhs, (((0,), (0,)), ((), ())), preferred_element_type=f32)
        for k in range(OUT_TILE // BLOCK):
            r = i * (OUT_TILE // BLOCK) + k
            part = slice(k * BLOCK, (k + 1) * BLOCK)
            held[i, part, :] = (total[part, :] * mask_ref[r : r + 1, :]).astype(bf16)
        leave(i).start()
    for i in range(tiles):
        leave(i).wait()


def weight_grad(acts, tokens, mask_scaled):
    f_local = acts[0].shape[1]
    every, d_local = 2 * tokens[0].shape[0], tokens[0].shape[1]
    vmem = pl.BlockSpec(memory_space=pltpu.VMEM)
    tiles = f_local // OUT_TILE
    return pl.pallas_call(
        weight_kernel,
        in_specs=[vmem] * 11,
        out_specs=pl.BlockSpec(memory_space=pl.ANY),
        scratch_shapes=[
            pltpu.VMEM((tiles, OUT_TILE, d_local), bf16),
            pltpu.SemaphoreType.DMA((tiles,)),
        ],
        out_shape=jax.ShapeDtypeStruct((f_local, d_local), bf16),
        compiler_params=pltpu.CompilerParams(vmem_limit_bytes=WEIGHT_VMEM),
        cost_estimate=pl.CostEstimate(
            flops=2 * every * f_local * d_local, bytes_accessed=2 * f_local * d_local, transcendentals=0
        ),
        name="weight_grad",
    )(*acts, *tokens, mask_scaled)


def tail_kernel(stay, got, last, gate, up, gate_out, up_out, by_gate, by_up, sems):
    width = stay.shape[1]
    step = width // TAIL_STEPS

    def leave(i):
        at = pl.ds(i * step, step)
        return (
            pltpu.make_async_copy(by_gate.at[:, at], gate_out.at[:, at], sems.at[0, i]),
            pltpu.make_async_copy(by_up.at[:, at], up_out.at[:, at], sems.at[1, i]),
        )

    for i in range(TAIL_STEPS):
        at = slice(i * step, (i + 1) * step)
        dact = stay[:, at].astype(f32) + got[:, at].astype(f32) + last[:, at].astype(f32)
        g, u = gate[:, at].astype(f32), up[:, at].astype(f32)
        sig = jax.nn.sigmoid(g)
        by_gate[:, at] = (dact * u * sig * (1.0 + g * (1.0 - sig))).astype(bf16)
        by_up[:, at] = (dact * g * sig).astype(bf16)
        for copy in leave(i):
            copy.start()
    for i in range(TAIL_STEPS):
        for copy in leave(i):
            copy.wait()


def tail_grads(stay, got, last, gate, up):
    vmem, anywhere = pl.BlockSpec(memory_space=pltpu.VMEM), pl.BlockSpec(memory_space=pl.ANY)
    like = jax.ShapeDtypeStruct(gate.shape, bf16)
    return pl.pallas_call(
        tail_kernel,
        in_specs=[vmem] * 5,
        out_specs=[anywhere] * 2,
        out_shape=[like] * 2,
        scratch_shapes=[pltpu.VMEM(gate.shape, bf16)] * 2
        + [pltpu.SemaphoreType.DMA((2, TAIL_STEPS))],
        compiler_params=pltpu.CompilerParams(vmem_limit_bytes=2 * SMALL_VMEM),
        name="activation_grads",
    )(stay, got, last, gate, up)


def activation(gate, up):
    gate, up = gate.astype(f32), up.astype(f32)
    return (gate * jax.nn.sigmoid(gate) * up).astype(bf16)


def local(grad_out, gate_pre, up_pre, w_down, block_mask):
    f_local, d_local = w_down.shape
    row, col = lax.axis_index("row"), lax.axis_index("col")
    scale = 1.0 / jnp.sqrt(f32(lax.axis_size("dp") * lax.axis_size("row") * grad_out.shape[1]))
    own_mask = lax.dynamic_slice(
        block_mask,
        (row * (f_local // BLOCK), col * (d_local // BLOCK)),
        (f_local // BLOCK, d_local // BLOCK),
    )
    keep = jnp.repeat((own_mask > 0).astype(f32), BLOCK, axis=1)
    keep_scaled = keep * scale

    gate, up = gate_pre[0], up_pre[0]
    own = grad_out[0]
    rows = own.shape[0]

    grads = [own] + [swap(own, "row", s) for s in (1, 2, 3)]
    act = activation(gate, up)
    act_x, act_y = swap(act, "dp", 1), swap(act, "col", 2)

    pos = jnp.full((1,), row ^ col, jnp.int32)
    tokens = stack(pos, grads)
    head, mark = fetch(w_down)
    tokens, keep, keep_scaled, mark = lax.optimization_barrier(
        (tokens, keep, keep_scaled, mark)
    )

    tokens_x, act_xy = swap(tokens, "dp", 1), swap(act_x, "col", 2)
    tokens, act, act_y, act_x, keep, mark = lax.optimization_barrier(
        (tokens, act, act_y, act_x, keep, mark)
    )
    stay, onward, send, send_next = partial_sums(tokens, keep, head, mark, w_down)
    send_next, tokens_x, act_xy = lax.optimization_barrier((send_next, tokens_x, act_xy))

    got_next = swap(send_next, "col", 1)
    act_c, act_yc, act_xc, act_xyc = [swap(a, "col", 1) for a in (act, act_y, act_x, act_xy)]
    theirs = (onward.astype(f32) + got_next.astype(f32)).astype(bf16)
    last = swap(theirs, "col", 2)
    send, act_xyc = lax.optimization_barrier((send, act_xyc))
    got = swap(send, "col", 1)

    acts = [act, act_y, act_c, act_yc, act_x, act_xy, act_xc, act_xyc]
    grad_down = weight_grad(acts, [tokens, tokens_x], keep_scaled)

    grad_gate, grad_up = tail_grads(stay, got, last, gate, up)
    return grad_gate[None], grad_up[None], grad_down


def general(grad_out, gate_pre, up_pre, w_down, block_mask):
    f_local, d_local = w_down.shape
    row_block = (lax.axis_index("row") * f_local + jnp.arange(f_local)) // BLOCK
    col_block = (lax.axis_index("col") * d_local + jnp.arange(d_local)) // BLOCK
    keep = block_mask[row_block][:, col_block] > 0
    w_kept = jnp.where(keep, w_down, jnp.zeros_like(w_down))
    gate, up = gate_pre[0].astype(f32), up_pre[0].astype(f32)
    sig = jax.nn.sigmoid(gate)
    act = (gate * sig * up).astype(bf16)
    grads = lax.all_gather(grad_out[0], "row", axis=0, tiled=True)
    partial = lax.dot_general(
        grads, w_kept, (((1,), (1,)), ((), ())), preferred_element_type=f32
    ).astype(bf16)
    dact = lax.psum_scatter(partial, "col", scatter_dimension=0, tiled=True).astype(f32)
    acts = lax.all_gather(act, ("dp", "col"), axis=0, tiled=True)
    every = lax.all_gather(grads, "dp", axis=0, tiled=True)
    total = lax.dot_general(acts, every, (((0,), (0,)), ((), ())), preferred_element_type=f32)
    scale = 1.0 / jnp.sqrt(f32(every.shape[0]))
    grad_down = jnp.where(keep, total * scale, jnp.zeros_like(total)).astype(bf16)
    grad_gate = (dact * up * sig * (1.0 + gate * (1.0 - sig))).astype(bf16)
    grad_up = (dact * gate * sig).astype(bf16)
    return grad_gate[None], grad_up[None], grad_down


def solution(mesh):
    placed = (
        P("dp", "row", "col"),
        P("dp", "col", "row"),
        P("dp", "col", "row"),
        P("row", "col"),
        P(),
    )
    size = dict(mesh.shape)
    pairwise = size["row"] == 4 and size["col"] == 4 and size["dp"] == 2

    def run(grad_out, gate_pre, up_pre, w_down, block_mask):
        f_local, d_local = w_down.shape
        rows = grad_out.shape[1]
        fits = pairwise and rows == gate_pre.shape[1] and rows % 16 == 0
        fits = fits and f_local % 1024 == 0 and d_local % BLOCK == 0
        step = local if fits else general
        return step(grad_out, gate_pre, up_pre, w_down, block_mask)

    return jax.shard_map(
        run,
        mesh=mesh,
        in_specs=placed,
        out_specs=(P("dp", "col", "row"), P("dp", "col", "row"), P("row", "col")),
        check_vma=False,
    )
```

```python
import jax
import jax.numpy as jnp
from jax import lax
from jax.experimental import pallas as pl
from jax.experimental.pallas import tpu as pltpu
from jax.sharding import PartitionSpec as P

BLOCK = 128
SUB = 256
IN_TILE = 512
TAIL_STEPS = 4
HEAD = 8
OUT_TILE = 256
SMALL_VMEM = 4 * 1024 * 1024
PARTIAL_VMEM = 24 * 1024 * 1024
WEIGHT_VMEM = 48 * 1024 * 1024
bf16 = jnp.bfloat16
f32 = jnp.float32


def swap(x, axis, bit):
    n = lax.axis_size(axis)
    return lax.ppermute(x, axis, [(i, i ^ bit) for i in range(n)])


def dest_slot(v):
    return (v >> 1) | ((v & 1) << 1)


def stack_kernel(pos_ref, g0, g1, g2, g3, out_ref):
    rows = g0.shape[0]
    for s, g in enumerate((g0, g1, g2, g3)):
        at = pl.multiple_of(dest_slot(pos_ref[0] ^ s) * rows, rows)
        out_ref[pl.ds(at, rows), :] = g[...]


def stack(pos, grads):
    rows, d_local = grads[0].shape
    vmem = pl.BlockSpec(memory_space=pltpu.VMEM)
    return pl.pallas_call(
        stack_kernel,
        in_specs=[pl.BlockSpec(memory_space=pltpu.SMEM)] + [vmem] * 4,
        out_specs=vmem,
        out_shape=jax.ShapeDtypeStruct((4 * rows, d_local), bf16),
        compiler_params=pltpu.CompilerParams(vmem_limit_bytes=SMALL_VMEM),
        name="stack_tokens",
    )(pos, *grads)


def fetch_kernel(w_ref, held_ref, done_ref, sems):
    def enter(i):
        at = pl.ds(i * IN_TILE, IN_TILE)
        return pltpu.make_async_copy(w_ref.at[at, :], held_ref.at[at, :], sems.at[i])

    tiles = held_ref.shape[0] // IN_TILE
    for i in range(tiles):
        enter(i).start()
    done_ref[...] = jnp.zeros_like(done_ref)
    for i in range(tiles):
        enter(i).wait()


def fetch(w):
    rows = w.shape[0] // IN_TILE * HEAD // 14 * IN_TILE
    anywhere = pl.BlockSpec(memory_space=pl.ANY)
    return pl.pallas_call(
        fetch_kernel,
        in_specs=[anywhere],
        out_specs=[anywhere, pl.BlockSpec(memory_space=pltpu.VMEM)],
        scratch_shapes=[pltpu.SemaphoreType.DMA((rows // IN_TILE,))],
        out_shape=[pltpu.VMEM((rows, w.shape[1]), bf16), jax.ShapeDtypeStruct((8, BLOCK), f32)],
        compiler_params=pltpu.CompilerParams(vmem_limit_bytes=SMALL_VMEM),
        cost_estimate=pl.CostEstimate(flops=0, bytes_accessed=2 * rows * w.shape[1], transcendentals=0),
        name="fetch_weights",
    )(pltpu.with_memory_space_constraint(w, pltpu.HBM))


def partial_kernel(lhs, mask_ref, head_ref, _, w_ref, stay_ref, next_ref, send_ref, send_next_ref, held, sems):
    rows = stay_ref.shape[0]
    first = head_ref.shape[0]
    ends = [first + (w_ref.shape[0] - first) // 2, w_ref.shape[0]]

    def enter(i):
        start = ends[i - 1] if i else first
        return pltpu.make_async_copy(
            w_ref.at[pl.ds(start, ends[i] - start), :],
            held.at[pl.ds(start - first, ends[i] - start), :],
            sems.at[i],
        )

    for i in range(len(ends)):
        enter(i).start()
    for k in range(w_ref.shape[0] // SUB):
        parts = []
        for j in range(SUB // BLOCK):
            r = k * (SUB // BLOCK) + j
            if r * BLOCK < first:
                w = head_ref[r * BLOCK : (r + 1) * BLOCK, :]
            else:
                if r * BLOCK in [first] + ends[:-1]:
                    enter(([first] + ends).index(r * BLOCK)).wait()
                w = held[r * BLOCK - first : (r + 1) * BLOCK - first, :]
            parts.append(w * mask_ref[r : r + 1, :].astype(bf16))
        out = lax.dot_general(
            jnp.concatenate(parts, axis=0),
            lhs[...],
            (((1,), (1,)), ((), ())),
            preferred_element_type=f32,
        ).T.astype(bf16)
        at = slice(k * SUB, (k + 1) * SUB)
        stay_ref[:, at] = out[:rows]
        next_ref[:, at] = out[rows : 2 * rows]
        send_ref[:, at] = out[2 * rows : 3 * rows]
        send_next_ref[:, at] = out[3 * rows :]


def partial_sums(tokens, mask_rows, head, mark, w):
    f_local, d_local = w.shape
    rows = tokens.shape[0] // 4
    vmem = pl.BlockSpec(memory_space=pltpu.VMEM)
    return pl.pallas_call(
        partial_kernel,
        in_specs=[vmem] * 3 + [pl.BlockSpec(memory_space=pl.ANY)] * 2,
        out_specs=[vmem] * 4,
        scratch_shapes=[
            pltpu.VMEM((f_local - head.shape[0], d_local), bf16),
            pltpu.SemaphoreType.DMA((2,)),
        ],
        out_shape=[
            jax.ShapeDtypeStruct((rows, f_local), bf16),
        ]
        * 4,
        compiler_params=pltpu.CompilerParams(vmem_limit_bytes=PARTIAL_VMEM),
        cost_estimate=pl.CostEstimate(
            flops=2 * 4 * rows * f_local * d_local, bytes_accessed=2 * f_local * d_local, transcendentals=0
        ),
        name="partial_sums",
    )(
        tokens,
        mask_rows,
        pltpu.with_memory_space_constraint(head, pltpu.VMEM),
        mark,
        pltpu.with_memory_space_constraint(w, pltpu.HBM),
    )


def weight_kernel(*refs):
    acts, tokens = refs[:8], refs[8:10]
    mask_ref, out_ref, held, sems = refs[10:]
    f_local = acts[0].shape[1]
    tiles = f_local // OUT_TILE

    def leave(i):
        return pltpu.make_async_copy(
            held.at[i], out_ref.at[pl.ds(i * OUT_TILE, OUT_TILE), :], sems.at[i]
        )

    rhs = jnp.concatenate([t[...] for t in tokens], axis=0)
    for i in range(tiles):
        at = slice(i * OUT_TILE, (i + 1) * OUT_TILE)
        lhs = jnp.concatenate([a[:, at] for a in acts], axis=0)
        total = lax.dot_general(lhs, rhs, (((0,), (0,)), ((), ())), preferred_element_type=f32)
        for k in range(OUT_TILE // BLOCK):
            r = i * (OUT_TILE // BLOCK) + k
            part = slice(k * BLOCK, (k + 1) * BLOCK)
            held[i, part, :] = (total[part, :] * mask_ref[r : r + 1, :]).astype(bf16)
        leave(i).start()
    for i in range(tiles):
        leave(i).wait()


def weight_grad(acts, tokens, mask_scaled):
    f_local = acts[0].shape[1]
    every, d_local = 2 * tokens[0].shape[0], tokens[0].shape[1]
    vmem = pl.BlockSpec(memory_space=pltpu.VMEM)
    tiles = f_local // OUT_TILE
    return pl.pallas_call(
        weight_kernel,
        in_specs=[vmem] * 11,
        out_specs=pl.BlockSpec(memory_space=pl.ANY),
        scratch_shapes=[
            pltpu.VMEM((tiles, OUT_TILE, d_local), bf16),
            pltpu.SemaphoreType.DMA((tiles,)),
        ],
        out_shape=jax.ShapeDtypeStruct((f_local, d_local), bf16),
        compiler_params=pltpu.CompilerParams(vmem_limit_bytes=WEIGHT_VMEM),
        cost_estimate=pl.CostEstimate(
            flops=2 * every * f_local * d_local, bytes_accessed=2 * f_local * d_local, transcendentals=0
        ),
        name="weight_grad",
    )(*acts, *tokens, mask_scaled)


def tail_kernel(stay, got, last, gate, up, gate_out, up_out, by_gate, by_up, sems):
    width = stay.shape[1]
    step = width // TAIL_STEPS

    def leave(i):
        at = pl.ds(i * step, step)
        return (
            pltpu.make_async_copy(by_gate.at[:, at], gate_out.at[:, at], sems.at[0, i]),
            pltpu.make_async_copy(by_up.at[:, at], up_out.at[:, at], sems.at[1, i]),
        )

    for i in range(TAIL_STEPS):
        at = slice(i * step, (i + 1) * step)
        dact = stay[:, at].astype(f32) + got[:, at].astype(f32) + last[:, at].astype(f32)
        g, u = gate[:, at].astype(f32), up[:, at].astype(f32)
        sig = jax.nn.sigmoid(g)
        by_gate[:, at] = (dact * u * sig * (1.0 + g * (1.0 - sig))).astype(bf16)
        by_up[:, at] = (dact * g * sig).astype(bf16)
        for copy in leave(i):
            copy.start()
    for i in range(TAIL_STEPS):
        for copy in leave(i):
            copy.wait()


def tail_grads(stay, got, last, gate, up):
    vmem, anywhere = pl.BlockSpec(memory_space=pltpu.VMEM), pl.BlockSpec(memory_space=pl.ANY)
    like = jax.ShapeDtypeStruct(gate.shape, bf16)
    return pl.pallas_call(
        tail_kernel,
        in_specs=[vmem] * 5,
        out_specs=[anywhere] * 2,
        out_shape=[like] * 2,
        scratch_shapes=[pltpu.VMEM(gate.shape, bf16)] * 2
        + [pltpu.SemaphoreType.DMA((2, TAIL_STEPS))],
        compiler_params=pltpu.CompilerParams(vmem_limit_bytes=2 * SMALL_VMEM),
        name="activation_grads",
    )(stay, got, last, gate, up)


def activation(gate, up):
    gate, up = gate.astype(f32), up.astype(f32)
    return (gate * jax.nn.sigmoid(gate) * up).astype(bf16)


def local(grad_out, gate_pre, up_pre, w_down, block_mask):
    f_local, d_local = w_down.shape
    row, col = lax.axis_index("row"), lax.axis_index("col")
    scale = 1.0 / jnp.sqrt(f32(lax.axis_size("dp") * lax.axis_size("row") * grad_out.shape[1]))
    own_mask = lax.dynamic_slice(
        block_mask,
        (row * (f_local // BLOCK), col * (d_local // BLOCK)),
        (f_local // BLOCK, d_local // BLOCK),
    )
    keep = jnp.repeat((own_mask > 0).astype(f32), BLOCK, axis=1)
    keep_scaled = keep * scale

    gate, up = gate_pre[0], up_pre[0]
    own = grad_out[0]
    rows = own.shape[0]

    grads = [own] + [swap(own, "row", s) for s in (1, 2, 3)]
    act = activation(gate, up)
    act_x, act_y = swap(act, "dp", 1), swap(act, "col", 2)

    pos = jnp.full((1,), row ^ col, jnp.int32)
    tokens = stack(pos, grads)
    head, mark = fetch(w_down)
    tokens, keep, keep_scaled, mark = lax.optimization_barrier(
        (tokens, keep, keep_scaled, mark)
    )

    tokens_x, act_xy = swap(tokens, "dp", 1), swap(act_x, "col", 2)
    tokens, act, act_y, act_x, keep, mark = lax.optimization_barrier(
        (tokens, act, act_y, act_x, keep, mark)
    )
    act_c = swap(act, "col", 1)
    stay, onward, send, send_next = partial_sums(tokens, keep, head, mark, w_down)
    send_next, tokens_x, act_xy, act_c = lax.optimization_barrier(
        (send_next, tokens_x, act_xy, act_c)
    )

    got_next = swap(send_next, "col", 1)
    act_yc = swap(act_y, "col", 1)
    act_xc = swap(act_x, "col", 1)
    act_xyc = swap(act_xy, "col", 1)
    theirs = (onward.astype(f32) + got_next.astype(f32)).astype(bf16)
    last = swap(theirs, "col", 2)
    send, act_xyc = lax.optimization_barrier((send, act_xyc))
    got = swap(send, "col", 1)

    acts = [act, act_y, act_c, act_yc, act_x, act_xy, act_xc, act_xyc]
    grad_down = weight_grad(acts, [tokens, tokens_x], keep_scaled)

    grad_gate, grad_up = tail_grads(stay, got, last, gate, up)
    return grad_gate[None], grad_up[None], grad_down


def general(grad_out, gate_pre, up_pre, w_down, block_mask):
    f_local, d_local = w_down.shape
    row_block = (lax.axis_index("row") * f_local + jnp.arange(f_local)) // BLOCK
    col_block = (lax.axis_index("col") * d_local + jnp.arange(d_local)) // BLOCK
    keep = block_mask[row_block][:, col_block] > 0
    w_kept = jnp.where(keep, w_down, jnp.zeros_like(w_down))
    gate, up = gate_pre[0].astype(f32), up_pre[0].astype(f32)
    sig = jax.nn.sigmoid(gate)
    act = (gate * sig * up).astype(bf16)
    grads = lax.all_gather(grad_out[0], "row", axis=0, tiled=True)
    partial = lax.dot_general(
        grads, w_kept, (((1,), (1,)), ((), ())), preferred_element_type=f32
    ).astype(bf16)
    dact = lax.psum_scatter(partial, "col", scatter_dimension=0, tiled=True).astype(f32)
    acts = lax.all_gather(act, ("dp", "col"), axis=0, tiled=True)
    every = lax.all_gather(grads, "dp", axis=0, tiled=True)
    total = lax.dot_general(acts, every, (((0,), (0,)), ((), ())), preferred_element_type=f32)
    scale = 1.0 / jnp.sqrt(f32(every.shape[0]))
    grad_down = jnp.where(keep, total * scale, jnp.zeros_like(total)).astype(bf16)
    grad_gate = (dact * up * sig * (1.0 + gate * (1.0 - sig))).astype(bf16)
    grad_up = (dact * gate * sig).astype(bf16)
    return grad_gate[None], grad_up[None], grad_down


def solution(mesh):
    placed = (
        P("dp", "row", "col"),
        P("dp", "col", "row"),
        P("dp", "col", "row"),
        P("row", "col"),
        P(),
    )
    size = dict(mesh.shape)
    pairwise = size["row"] == 4 and size["col"] == 4 and size["dp"] == 2

    def run(grad_out, gate_pre, up_pre, w_down, block_mask):
        f_local, d_local = w_down.shape
        rows = grad_out.shape[1]
        fits = pairwise and rows == gate_pre.shape[1] and rows % 16 == 0
        fits = fits and f_local % 1024 == 0 and d_local % BLOCK == 0
        step = local if fits else general
        return step(grad_out, gate_pre, up_pre, w_down, block_mask)

    return jax.shard_map(
        run,
        mesh=mesh,
        in_specs=placed,
        out_specs=(P("dp", "col", "row"), P("dp", "col", "row"), P("row", "col")),
        check_vma=False,
    )
```
